32 devices in a mesh: groups: 2 (over x), hst: 2 (over core), local: 8 (over z, y).
Axes of the slice: x: 2, y: 2, z: 4, core: 2. Of those that a mesh axis runs over, the one named last changes fastest.
Arguments:
- tokens: bfloat16 [4096, 7168], P(('groups', 'hst', 'local')), parts along dimension 0, may hold values from -6 to 6
- expert_ids: int32 [4096, 8], P(('groups', 'hst', 'local')), parts along dimension 0, may hold values from 0 to 255, as said below
- route_weights: float32 [4096, 8], P(('groups', 'hst', 'local')), parts along dimension 0, may hold values from 0.1 to 1
- gate_weight: bfloat16 [7168, 2048], P(None, ('hst', 'local')), may hold values from -0.0625 to 0.0625
- up_weight: bfloat16 [7168, 2048], P(None, ('hst', 'local')), may hold values from -0.0625 to 0.0625
- down_weight: bfloat16 [2048, 7168], P(('hst', 'local')), may hold values from -0.1875 to 0.1875
Outputs:
- routed: bfloat16 [4096, 7168], P(('groups', 'hst', 'local')), parts along dimension 0
The draws below stay inside these ranges and needn't reach their ends.
There are 2 independent parts, one for each index of `groups`. The reference program is written for one: setup_inputs(seed, part) draws one part's arguments, and reference() takes and returns one part's arrays. A program takes and returns all parts, laid end to end along the dimension named above; an argument that names none is the same for every part. Nothing has to cross between parts.
Inputs may be any that keep to these rules, and one draw needn't show every extreme that they name: `expert_ids`: each row names 8 different experts. The experts below 2 are the held ones; of the 128 rows of one device at most 6 name any one held expert. One held expert is named by exactly 6 rows of every device, and every other held expert by up to 6 rows.
All inputs are finite; a program needn't handle non-finite values.
Results may differ from the reference program's by a relative error of at most 0.0057.
Values may be sent and summed in bfloat16 or wider, within the bound.
No kernel may reach another device: no remote copies, remote signals or barrier semaphores. Data moves between devices by JAX's collectives and lax.ppermute only.
A program may use at most 64 MiB of HBM per device.

```python
import jax
import jax.numpy as jnp
from jax import lax

D = 7168
FF = 1024
EXPERTS = 256
TOPK = 8
SPLIT = 8
TOK_DEV = 128
W = 2
MOST = 6
TOKENS = 2048
N_HST = 2
N_LOCAL = 8


def draw_expert_ids(key, part):
    key = jax.random.fold_in(key, 17)
    key_hot, key_second, key_count, key_rank, key_other, key_order = jax.random.split(key, 6)
    blocks = TOKENS // TOK_DEV
    common = jax.random.randint(key_hot, (), 0, W)
    second = jax.random.randint(key_second, (blocks,), 0, W)
    floor_count = max(1, MOST // 4)
    counts = jax.random.randint(key_count, (blocks, W), floor_count, MOST + 1)
    held_index = jnp.arange(W)[None, :]
    is_full = (held_index == common) | (held_index == second[:, None])
    counts = jnp.where(is_full, MOST, counts)
    rank_keys = jax.random.split(key_rank, blocks * W)
    row_ranks = jax.vmap(lambda piece_key: jax.random.permutation(piece_key, TOK_DEV))(rank_keys).reshape(blocks, W, TOK_DEV)
    member = row_ranks < counts[:, :, None]
    member = jnp.transpose(member, (0, 2, 1)).reshape(TOKENS, W).astype(jnp.int32)
    window_count = jnp.sum(member, axis=1)
    rank_in_row = jnp.cumsum(member, axis=1) - 1
    columns = jnp.arange(TOPK)
    hit_slot = (member[:, None, :] == 1) & (rank_in_row[:, None, :] == columns[None, :, None])
    window = jnp.sum(jnp.where(hit_slot, jnp.arange(W)[None, None, :], 0), axis=2)
    other_keys = jax.random.split(key_other, TOKENS)
    outside = jax.vmap(lambda piece_key: jax.random.permutation(piece_key, EXPERTS - W)[:TOPK])(other_keys) + W
    shifted = jnp.clip(columns[None, :] - window_count[:, None], 0, TOPK - 1)
    outside = jnp.take_along_axis(outside, shifted, axis=1)
    ordered = jnp.where(columns[None, :] < window_count[:, None], window, outside)
    order_keys = jax.random.split(key_order, TOKENS)
    shuffle = jax.vmap(lambda piece_key: jax.random.permutation(piece_key, TOPK))(order_keys)
    return jnp.take_along_axis(ordered, shuffle, axis=1).astype(jnp.int32)


def block_scale(own_key, extent, cuts, low, top_value):
    factor_of = 1.0
    for dim, parts in cuts:
        heights = jax.random.uniform(jax.random.fold_in(jax.random.fold_in(own_key, 6), dim), (parts,), jnp.float32, low / len(cuts), top_value / len(cuts))
        factor_of = factor_of * jnp.repeat(jnp.exp(heights), extent[dim] // parts).reshape((-1,) + (1,) * (len(extent) - 1 - dim))
    return factor_of


def scatter_about(own_key, dims, scale, limit, shards=(), kind=jnp.bfloat16):
    result = jax.random.normal(own_key, dims, jnp.float32) * scale
    if len(shards) > 0:
        result = block_scale(own_key, dims, shards, -0.22, 0.18) * result
    return jnp.clip(result, min=-limit, max=limit).astype(kind)


def setup_inputs(seed: int = 0, part: int = 0) -> dict:
    arg_keys = jax.random.split(jax.random.key(seed), 7)
    own_keys = jax.random.split(jax.random.fold_in(arg_keys[6], part), 7)
    tokens = scatter_about(own_keys[0], (TOKENS, D), 1.0, 6.0, ((0, 16),))
    expert_ids = draw_expert_ids(jax.random.fold_in(jax.random.fold_in(arg_keys[6], part), 71), part)
    route_weights = jnp.clip(0.1 + 0.9 * jax.random.uniform(own_keys[2], (TOKENS, TOPK), jnp.float32) ** block_scale(own_keys[2], (TOKENS, TOPK), ((0, 16),), -0.2, 0.2), 0.1, 1.0)
    gate_weight = scatter_about(arg_keys[3], (D, W * FF), D ** -0.5, 0.0625, ((1, 16),))
    up_weight = scatter_about(arg_keys[4], (D, W * FF), D ** -0.5, 0.0625, ((1, 16),))
    down_weight = scatter_about(arg_keys[5], (W * FF, D), FF ** -0.5, 0.1875, ((0, 16),))
    return {"tokens": tokens, "expert_ids": expert_ids, "route_weights": route_weights, "gate_weight": gate_weight, "up_weight": up_weight, "down_weight": down_weight}


def reference(tokens, expert_ids, route_weights, gate_weight, up_weight, down_weight):
    experts_win = N_HST * N_LOCAL // SPLIT
    row_limit = N_HST * N_LOCAL * MOST
    unit_share = FF // SPLIT
    total = jnp.zeros((TOKENS, D), jnp.float32)
    for expert in range(experts_win):
        named = expert_ids == expert
        chosen = jnp.any(named, axis=1)
        weight = jnp.sum(jnp.where(named, route_weights, jnp.float32(0.0)), axis=1)
        (row_index,) = jnp.nonzero(chosen, size=row_limit, fill_value=0)
        row_index = row_index.astype(jnp.int32)
        is_valid = jnp.arange(row_limit) < jnp.sum(chosen.astype(jnp.int32))
        gathered = tokens[row_index]
        gathered = jnp.where(is_valid[:, None], gathered, jnp.zeros_like(gathered))
        start = expert * FF
        gate_sum = jnp.dot(gathered, gate_weight[:, start:start + FF], preferred_element_type=jnp.float32)
        up_sum = jnp.dot(gathered, up_weight[:, start:start + FF], preferred_element_type=jnp.float32)
        hidden = (jax.nn.silu(gate_sum) * up_sum).astype(jnp.bfloat16)
        down_rows = down_weight[start:start + FF].reshape(SPLIT, unit_share, D).astype(jnp.float32)
        pieces = jnp.einsum("nsf,sfd->nsd", hidden.reshape(row_limit, SPLIT, unit_share).astype(jnp.float32), down_rows, precision=lax.Precision.HIGHEST)
        pieces = lax.optimization_barrier(pieces.astype(jnp.bfloat16)).astype(jnp.float32)
        scale = jnp.where(is_valid, weight[row_index], jnp.float32(0.0))
        combined = jnp.sum(pieces, axis=1) * scale[:, None]
        total = total.at[row_index].add(combined)
    return total.astype(jnp.bfloat16)
```

```python
import jax
import jax.numpy as jnp
from jax import lax
from jax.experimental import pallas as pl
from jax.experimental.pallas import tpu as pltpu
from jax.sharding import PartitionSpec as P

SPLIT = 8
MOST = 6
SEGS = 4
ROWS = SEGS * MOST
BF = jnp.bfloat16
F32 = jnp.float32
VMEM_LIMIT = 48 * 1024 * 1024


def route_table(expert_ids, route_weights, experts_win):
    window = jnp.arange(experts_win, dtype=jnp.int32)
    matched = expert_ids[:, :, None] == window[None, None, :]
    is_hit = jnp.any(matched, axis=1).astype(jnp.int32)
    weight = jnp.sum(jnp.where(matched, route_weights[:, :, None], F32(0.0)), axis=1)
    position = jnp.cumsum(is_hit, axis=0) - 1
    slot_index = jnp.arange(MOST, dtype=jnp.int32)
    select = (is_hit.T[:, None, :] == 1) & (position.T[:, None, :] == slot_index[None, :, None])
    return (select, weight)


def general(tokens, expert_ids, route_weights, gate_weight, up_weight, down_weight):
    host_count = lax.axis_size("hst")
    local_count = lax.axis_size("local")
    per_host = local_count // SPLIT
    experts_win = host_count * per_host
    width = tokens.shape[1]
    select, weight = route_table(expert_ids, route_weights, experts_win)
    outgoing = jnp.einsum(
        "wmt,td->wmd", select.astype(BF), tokens, preferred_element_type=F32
    ).astype(BF)
    slot_weight = jnp.einsum(
        "wmt,tw->wm", select.astype(F32), weight, precision=lax.Precision.HIGHEST
    )
    host_rows = lax.all_to_all(
        outgoing.reshape(host_count, per_host, MOST, width), "hst", 0, 0, tiled=True
    )
    spread = jnp.repeat(jnp.transpose(host_rows, (1, 0, 2, 3)), SPLIT, axis=0)
    row_block = lax.all_to_all(spread, "local", 0, 0, tiled=True)
    in_shape = row_block.shape
    flattened = row_block.reshape(-1, width)
    gate_sum = jnp.dot(flattened, gate_weight, preferred_element_type=F32)
    up_sum = jnp.dot(flattened, up_weight, preferred_element_type=F32)
    hidden = (jax.nn.silu(gate_sum) * up_sum).astype(BF)
    partial_value = jnp.dot(hidden, down_weight, preferred_element_type=F32).astype(BF)
    partial_value = partial_value.reshape(in_shape)
    returned_rows = lax.all_to_all(partial_value, "local", 0, 0, tiled=True)
    summed = jnp.sum(
        returned_rows.reshape(per_host, SPLIT, host_count, MOST, width).astype(F32), axis=1
    )
    returned_sums = lax.all_to_all(
        jnp.transpose(summed, (1, 0, 2, 3)), "hst", 0, 0, tiled=True
    )
    combined = returned_sums.reshape(experts_win, MOST, width)
    weighted = combined * slot_weight[:, :, None]
    total = jnp.einsum(
        "wmt,wmd->td", select.astype(F32), weighted, precision=lax.Precision.HIGHEST
    )
    return total.astype(BF)


def select_rows(core, tokens, ids_t, weights_t):
    count, width = tokens.shape
    seg = width // SEGS
    topk = ids_t.shape[0]

    def kernel(core_ref, ids_ref, weights_ref, tokens_ref, own_ref, twin_ref, slot_ref, scale_ref, acc):
        step = pl.program_id(0)

        @pl.when(step == 0)
        def _():
            core = core_ref[0]
            ids = ids_ref[...]
            row = lax.broadcasted_iota(jnp.int32, (count, count), 0)
            col = lax.broadcasted_iota(jnp.int32, (count, count), 1)
            before = (row < col).astype(BF)
            slot = lax.broadcasted_iota(jnp.int32, (ROWS, count), 0) % MOST
            for part in range(2):
                expert = core if part == 0 else 1 - core
                named = ids == expert
                hit = jnp.max(named.astype(F32), axis=0, keepdims=True)
                weight = jnp.sum(jnp.where(named, weights_ref[...], 0.0), axis=0, keepdims=True)
                wide = jnp.broadcast_to(hit, (16, count)).astype(BF)
                position = jnp.dot(wide, before, preferred_element_type=F32)[0:1]
                chosen = (hit > 0.0) & (position.astype(jnp.int32) == slot)
                table = chosen.astype(F32)
                slot_ref[part] = table
                scale = jnp.sum(table * weight, axis=1, keepdims=True)
                scale_ref[part] = jnp.broadcast_to(scale, (ROWS, 128))

        line = lax.broadcasted_iota(jnp.int32, (ROWS, count), 0) // MOST
        keep = line == step
        table = jnp.concatenate(
            [jnp.where(keep, slot_ref[0], 0.0), jnp.where(keep, slot_ref[1], 0.0)], axis=0
        ).astype(BF)
        rows = jnp.dot(table, tokens_ref[...], preferred_element_type=F32)

        @pl.when(step == 0)
        def _():
            acc[...] = rows

        @pl.when(step > 0)
        def _():
            acc[...] += rows

        @pl.when(step == SEGS - 1)
        def _():
            own_ref[...] = acc[0:ROWS].astype(BF)
            twin_ref[...] = acc[ROWS : 2 * ROWS].astype(BF)

    whole = lambda *shape: pl.BlockSpec(shape, lambda i, *_: (0,) * len(shape))
    return pl.pallas_call(
        kernel,
        grid_spec=pltpu.PrefetchScalarGridSpec(
            num_scalar_prefetch=1,
            grid=(SEGS,),
            in_specs=[
                whole(topk, count),
                whole(topk, count),
                pl.BlockSpec((count, seg), lambda i, *_: (0, i)),
            ],
            out_specs=[
                whole(ROWS, seg),
                whole(ROWS, seg),
                whole(2, ROWS, count),
                whole(2, ROWS, 128),
            ],
            scratch_shapes=[pltpu.VMEM((2 * ROWS, seg), F32)],
        ),
        out_shape=[
            jax.ShapeDtypeStruct((ROWS, seg), BF),
            jax.ShapeDtypeStruct((ROWS, seg), BF),
            jax.ShapeDtypeStruct((2, ROWS, count), F32),
            jax.ShapeDtypeStruct((2, ROWS, 128), F32),
        ],
        compiler_params=pltpu.CompilerParams(vmem_limit_bytes=VMEM_LIMIT),
        name="select_rows",
    )(core, ids_t, weights_t, tokens)


def experts(blocks, gate_weight, up_weight, down_weight):
    seg = blocks[0].shape[1]
    units = gate_weight.shape[1]
    height = SPLIT * ROWS
    tile = 256

    def kernel(*refs):
        block_refs = refs[:SPLIT]
        gate_ref, up_ref, down_ref, far_ref, near_ref, kept_ref = refs[SPLIT:]
        rows = jnp.concatenate([ref[...] for ref in block_refs], axis=0)
        line = lax.broadcasted_iota(jnp.int32, (height, 2 * units), 0) % ROWS // MOST
        total = jnp.zeros((height, 2 * units), F32)
        for s in range(SEGS):
            cut = slice(s * seg, (s + 1) * seg)
            both = jnp.concatenate([gate_ref[cut, :], up_ref[cut, :]], axis=1)
            part = jnp.dot(rows, both, preferred_element_type=F32)
            total = total + jnp.where(line == s, part, 0.0)
        one = lax.broadcasted_iota(jnp.int32, (height, height), 0)
        two = lax.broadcasted_iota(jnp.int32, (height, height), 1)
        same = (one // ROWS == two // ROWS) & (one % MOST == two % MOST)
        spread = jnp.dot(
            same.astype(F32), total, precision=lax.Precision.HIGHEST, preferred_element_type=F32
        )
        gate = spread[:, :units]
        up = spread[:, units:]
        hidden = gate / (1.0 + jnp.exp(-gate)) * up
        wide = jnp.concatenate(
            [jnp.where(line[:, :units] == s, hidden, 0.0) for s in range(SEGS)], axis=1
        ).astype(BF)
        for j in range(seg // tile):
            weights = jnp.concatenate(
                [down_ref[:, s * seg + j * tile : s * seg + (j + 1) * tile] for s in range(SEGS)],
                axis=0,
            )
            out = jnp.dot(wide, weights, preferred_element_type=F32).astype(BF)
            cut = slice(j * tile, (j + 1) * tile)
            far_ref[:, cut] = out[: 2 * ROWS]
            near_ref[:, cut] = out[2 * ROWS : 4 * ROWS]
            kept_ref[:, cut] = out[4 * ROWS :]

    return pl.pallas_call(
        kernel,
        in_specs=[pl.BlockSpec(memory_space=pltpu.VMEM)] * (SPLIT + 3),
        out_specs=[pl.BlockSpec(memory_space=pltpu.VMEM)] * 3,
        out_shape=[
            jax.ShapeDtypeStruct((2 * ROWS, seg), BF),
            jax.ShapeDtypeStruct((2 * ROWS, seg), BF),
            jax.ShapeDtypeStruct((4 * ROWS, seg), BF),
        ],
        compiler_params=pltpu.CompilerParams(vmem_limit_bytes=VMEM_LIMIT),
        cost_estimate=pl.CostEstimate(
            flops=2 * height * seg * SEGS * units * 3,
            bytes_accessed=3 * 2 * units * seg * SEGS,
            transcendentals=0,
        ),
        name="experts",
    )(*blocks, gate_weight, up_weight, down_weight)


def combine(own_terms, twin, slot, scale):
    kept, near, others = own_terms
    seg = twin.shape[1]
    count = slot.shape[2]

    def kernel(kept_ref, near_ref, one_ref, two_ref, three_ref, twin_ref, slot_ref, scale_ref, out_ref, rows):
        step = pl.program_id(0)

        @pl.when(step == 0)
        def _():
            own = kept_ref[0:ROWS].astype(F32) + near_ref[ROWS : 2 * ROWS].astype(F32)
            own = own + one_ref[...].astype(F32)
            own = own + two_ref[...].astype(F32)
            own = own + three_ref[...].astype(F32)
            own = own * scale_ref[0][:, 0:1]
            other = twin_ref[...].astype(F32) * scale_ref[1][:, 0:1]
            both = jnp.concatenate([own, other], axis=0)
            high = both.astype(BF)
            low = (both - high.astype(F32)).astype(BF)
            rows[...] = jnp.concatenate([high, low], axis=0)

        line = lax.broadcasted_iota(jnp.int32, (ROWS, count), 0) // MOST
        keep = line == step
        table = jnp.concatenate(
            [jnp.where(keep, slot_ref[0], 0.0), jnp.where(keep, slot_ref[1], 0.0)], axis=0
        ).astype(BF)
        table = jnp.concatenate([table, table], axis=0)
        out_ref[...] = lax.dot_general(
            table, rows[...], (((0,), (0,)), ((), ())), preferred_element_type=F32
        ).astype(BF)

    whole = lambda *shape: pl.BlockSpec(shape, lambda i: (0,) * len(shape))
    operands = (kept, near, *others, twin, slot, scale)
    return pl.pallas_call(
        kernel,
        grid=(SEGS,),
        in_specs=[whole(*x.shape) for x in operands],
        out_specs=pl.BlockSpec((count, seg), lambda i: (0, i)),
        out_shape=jax.ShapeDtypeStruct((count, seg * SEGS), BF),
        scratch_shapes=[pltpu.VMEM((4 * ROWS, seg), BF)],
        compiler_params=pltpu.CompilerParams(vmem_limit_bytes=VMEM_LIMIT),
        name="combine",
    )(*operands)


def swap(x, mask):
    return lax.ppermute(x, "local", [(i, i ^ mask) for i in range(SPLIT)])


def swap_cores(x):
    return lax.ppermute(x, "hst", [(0, 1), (1, 0)])


def gather(block):
    got = {0: block}
    got[1] = swap(block, 1)
    got[4] = swap(block, 4)
    got[6] = swap(block, 6)
    got[2] = swap(block, 2)
    for k in (2, 4, 6):
        got[k + 1] = swap(got[k], 1)
    return got


def scatter(far, near, kept):
    far = swap(far, 1)
    near = swap(near, 1)
    add = lambda a, b: (a.astype(F32) + b.astype(F32)).astype(BF)
    four = swap(add(kept[2 * ROWS : 3 * ROWS], far[:ROWS]), 4)
    six = swap(add(kept[3 * ROWS :], far[ROWS:]), 6)
    two = swap(add(kept[ROWS : 2 * ROWS], near[:ROWS]), 2)
    return kept, near, (two, four, six)


def single(tokens, expert_ids, route_weights, gate_weight, up_weight, down_weight):
    core = lax.axis_index("hst").astype(jnp.int32).reshape(1)
    own, other, slot, scale = select_rows(core, tokens, expert_ids.T, route_weights.T)
    terms = []
    twin = swap_cores(other)
    for block in (own, twin):
        got = gather(block)
        order = [got[k] for k in (5, 7, 3, 1, 0, 2, 4, 6)]
        far, near, kept = experts(order, gate_weight, up_weight, down_weight)
        terms.append(scatter(far, near, kept))
    kept, near, others = terms[1]
    back = kept[:ROWS].astype(F32) + near[ROWS:].astype(F32)
    for x in others:
        back = back + x.astype(F32)
    back = swap_cores(back.astype(BF))
    return combine(terms[0], back, slot, scale)


def solution(mesh):
    in_specs = (
        P(("groups", "hst", "local"), None),
        P(("groups", "hst", "local"), None),
        P(("groups", "hst", "local"), None),
        P(None, ("hst", "local")),
        P(None, ("hst", "local")),
        P(("hst", "local"), None),
    )
    out_specs = P(("groups", "hst", "local"), None)
    body = single if mesh.shape["local"] == SPLIT and mesh.shape["hst"] == 2 else general
    return jax.shard_map(
        body, mesh=mesh, in_specs=in_specs, out_specs=out_specs, check_vma=False
    )
```

```python
import jax
import jax.numpy as jnp
from jax import lax
from jax.experimental import pallas as pl
from jax.experimental.pallas import tpu as pltpu
from jax.sharding import PartitionSpec as P

SPLIT = 8
MOST = 6
SEGS = 4
ROWS = SEGS * MOST
BF = jnp.bfloat16
F32 = jnp.float32
MIB = 1024 * 1024


def route_table(expert_ids, route_weights, experts_win):
    window = jnp.arange(experts_win, dtype=jnp.int32)
    matched = expert_ids[:, :, None] == window[None, None, :]
    is_hit = jnp.any(matched, axis=1).astype(jnp.int32)
    weight = jnp.sum(jnp.where(matched, route_weights[:, :, None], F32(0.0)), axis=1)
    position = jnp.cumsum(is_hit, axis=0) - 1
    slot_index = jnp.arange(MOST, dtype=jnp.int32)
    select = (is_hit.T[:, None, :] == 1) & (position.T[:, None, :] == slot_index[None, :, None])
    return (select, weight)


def general(tokens, expert_ids, route_weights, gate_weight, up_weight, down_weight):
    host_count = lax.axis_size("hst")
    local_count = lax.axis_size("local")
    per_host = local_count // SPLIT
    experts_win = host_count * per_host
    width = tokens.shape[1]
    select, weight = route_table(expert_ids, route_weights, experts_win)
    outgoing = jnp.einsum(
        "wmt,td->wmd", select.astype(BF), tokens, preferred_element_type=F32
    ).astype(BF)
    slot_weight = jnp.einsum(
        "wmt,tw->wm", select.astype(F32), weight, precision=lax.Precision.HIGHEST
    )
    host_rows = lax.all_to_all(
        outgoing.reshape(host_count, per_host, MOST, width), "hst", 0, 0, tiled=True
    )
    spread = jnp.repeat(jnp.transpose(host_rows, (1, 0, 2, 3)), SPLIT, axis=0)
    row_block = lax.all_to_all(spread, "local", 0, 0, tiled=True)
    in_shape = row_block.shape
    flattened = row_block.reshape(-1, width)
    gate_sum = jnp.dot(flattened, gate_weight, preferred_element_type=F32)
    up_sum = jnp.dot(flattened, up_weight, preferred_element_type=F32)
    hidden = (jax.nn.silu(gate_sum) * up_sum).astype(BF)
    partial_value = jnp.dot(hidden, down_weight, preferred_element_type=F32).astype(BF)
    partial_value = partial_value.reshape(in_shape)
    returned_rows = lax.all_to_all(partial_value, "local", 0, 0, tiled=True)
    summed = jnp.sum(
        returned_rows.reshape(per_host, SPLIT, host_count, MOST, width).astype(F32), axis=1
    )
    returned_sums = lax.all_to_all(
        jnp.transpose(summed, (1, 0, 2, 3)), "hst", 0, 0, tiled=True
    )
    combined = returned_sums.reshape(experts_win, MOST, width)
    weighted = combined * slot_weight[:, :, None]
    total = jnp.einsum(
        "wmt,wmd->td", select.astype(F32), weighted, precision=lax.Precision.HIGHEST
    )
    return total.astype(BF)


def in_hbm(x):
    return pltpu.with_memory_space_constraint(x, pltpu.HBM)


def join(*arrays):
    many = len(arrays)

    def kernel(*refs):
        pass

    return pl.pallas_call(
        kernel,
        in_specs=[pl.BlockSpec(memory_space=pltpu.VMEM)] * many,
        out_specs=[pl.BlockSpec(memory_space=pltpu.VMEM)] * many,
        out_shape=[jax.ShapeDtypeStruct(x.shape, x.dtype) for x in arrays],
        input_output_aliases={i: i for i in range(many)},
        compiler_params=pltpu.CompilerParams(vmem_limit_bytes=8 * MIB),
        name="join",
    )(*arrays)


def load_weights(gate_weight, up_weight, down_weight):
    width, units = gate_weight.shape
    seg = width // SEGS

    def kernel(gate_hbm, up_hbm, down_hbm, both_ref, down_ref, sems):
        copies = [
            pltpu.make_async_copy(gate_hbm, both_ref.at[:, pl.ds(0, units)], sems.at[0]),
            pltpu.make_async_copy(up_hbm, both_ref.at[:, pl.ds(units, units)], sems.at[1]),
        ]
        for s in range(SEGS):
            copies.append(
                pltpu.make_async_copy(
                    down_hbm.at[:, pl.ds(s * seg, seg)],
                    down_ref.at[pl.ds(s * units, units), :],
                    sems.at[2 + s],
                )
            )
        for copy in copies:
            copy.start()
        for copy in copies:
            copy.wait()

    return pl.pallas_call(
        kernel,
        in_specs=[pl.BlockSpec(memory_space=pltpu.HBM)] * 3,
        out_specs=[pl.BlockSpec(memory_space=pltpu.VMEM)] * 2,
        out_shape=[
            jax.ShapeDtypeStruct((width, 2 * units), BF),
            jax.ShapeDtypeStruct((SEGS * units, seg), BF),
        ],
        scratch_shapes=[pltpu.SemaphoreType.DMA((2 + SEGS,))],
        compiler_params=pltpu.CompilerParams(vmem_limit_bytes=12 * MIB),
        name="load_weights",
    )(*[in_hbm(x) for x in (gate_weight, up_weight, down_weight)])


def select_rows(core, tokens, ids_t, weights_t):
    count, width = tokens.shape
    seg = width // SEGS
    topk = ids_t.shape[0]

    def kernel(
        core_ref, ids_hbm, weights_hbm, tokens_hbm,
        own_ref, twin_ref, slot_ref, scale_ref,
        ids_ref, weights_ref, tokens_ref, small_sem, sems,
    ):
        first = pltpu.make_async_copy(ids_hbm, ids_ref, small_sem.at[0])
        second = pltpu.make_async_copy(weights_hbm, weights_ref, small_sem.at[1])
        first.start()
        second.start()
        copies = [
            pltpu.make_async_copy(
                tokens_hbm.at[:, pl.ds(s * seg, seg)], tokens_ref.at[s], sems.at[s]
            )
            for s in range(SEGS)
        ]
        for copy in copies:
            copy.start()
        core = core_ref[0]
        row = lax.broadcasted_iota(jnp.int32, (count, count), 0)
        col = lax.broadcasted_iota(jnp.int32, (count, count), 1)
        before = (row < col).astype(BF)
        slot = lax.broadcasted_iota(jnp.int32, (ROWS, count), 0) % MOST
        line = lax.broadcasted_iota(jnp.int32, (2 * ROWS, count), 0) % ROWS // MOST
        first.wait()
        second.wait()
        ids = ids_ref[...]
        tables = []
        for part in range(2):
            expert = core if part == 0 else 1 - core
            named = ids == expert
            hit = jnp.max(named.astype(F32), axis=0, keepdims=True)
            weight = jnp.sum(jnp.where(named, weights_ref[...], 0.0), axis=0, keepdims=True)
            wide = jnp.broadcast_to(hit, (16, count)).astype(BF)
            position = jnp.dot(wide, before, preferred_element_type=F32)[0:1]
            table = ((hit > 0.0) & (position.astype(jnp.int32) == slot)).astype(F32)
            slot_ref[part] = table
            scale = jnp.sum(table * weight, axis=1, keepdims=True)
            scale_ref[part] = jnp.broadcast_to(scale, (ROWS, 128))
            tables.append(table)
        table = jnp.concatenate(tables, axis=0)
        rows = jnp.zeros((2 * ROWS, seg), F32)
        for s in range(SEGS):
            copies[s].wait()
            chosen = jnp.where(line == s, table, 0.0).astype(BF)
            rows = rows + jnp.dot(chosen, tokens_ref[s], preferred_element_type=F32)
        own_ref[...] = rows[:ROWS].astype(BF)
        twin_ref[...] = rows[ROWS:].astype(BF)

    return pl.pallas_call(
        kernel,
        in_specs=[pl.BlockSpec(memory_space=pltpu.SMEM)] + [pl.BlockSpec(memory_space=pltpu.HBM)] * 3,
        out_specs=[pl.BlockSpec(memory_space=pltpu.VMEM)] * 4,
        out_shape=[
            jax.ShapeDtypeStruct((ROWS, seg), BF),
            jax.ShapeDtypeStruct((ROWS, seg), BF),
            jax.ShapeDtypeStruct((2, ROWS, count), F32),
            jax.ShapeDtypeStruct((2, ROWS, 128), F32),
        ],
        scratch_shapes=[
            pltpu.VMEM((topk, count), jnp.int32),
            pltpu.VMEM((topk, count), F32),
            pltpu.VMEM((SEGS, count, seg), BF),
            pltpu.SemaphoreType.DMA((2,)),
            pltpu.SemaphoreType.DMA((SEGS,)),
        ],
        compiler_params=pltpu.CompilerParams(vmem_limit_bytes=12 * MIB),
        name="select_rows",
    )(core, *[in_hbm(x) for x in (ids_t, weights_t, tokens)])


def experts(blocks, both_weight, down_weight):
    many = len(blocks)
    tall, seg = blocks[0].shape
    units = both_weight.shape[1] // 2
    height = many * tall
    tile = 256

    def kernel(*refs):
        block_refs = refs[:many]
        both_ref, down_ref = refs[many : many + 2]
        out_refs = refs[many + 2 :]
        rows = jnp.concatenate([ref[...] for ref in block_refs], axis=0)
        line = lax.broadcasted_iota(jnp.int32, (height, 2 * units), 0) % ROWS // MOST
        total = jnp.zeros((height, 2 * units), F32)
        for s in range(SEGS):
            cut = slice(s * seg, (s + 1) * seg)
            part = jnp.dot(rows, both_ref[cut, :], preferred_element_type=F32)
            total = total + jnp.where(line == s, part, 0.0)
        one = lax.broadcasted_iota(jnp.int32, (tall, tall), 0)
        two = lax.broadcasted_iota(jnp.int32, (tall, tall), 1)
        same = ((one // ROWS == two // ROWS) & (one % MOST == two % MOST)).astype(F32)
        spread = jnp.concatenate(
            [
                jnp.dot(
                    same,
                    total[b * tall : (b + 1) * tall],
                    precision=lax.Precision.HIGHEST,
                    preferred_element_type=F32,
                )
                for b in range(many)
            ],
            axis=0,
        )
        gate = spread[:, :units]
        up = spread[:, units:]
        hidden = gate / (1.0 + jnp.exp(-gate)) * up
        wide = jnp.concatenate(
            [jnp.where(line[:, :units] == s, hidden, 0.0) for s in range(SEGS)], axis=1
        ).astype(BF)
        for j in range(seg // tile):
            cut = slice(j * tile, (j + 1) * tile)
            out = jnp.dot(wide, down_ref[:, cut], preferred_element_type=F32).astype(BF)
            for b in range(many):
                out_refs[b][:, cut] = out[b * tall : (b + 1) * tall]

    return pl.pallas_call(
        kernel,
        in_specs=[pl.BlockSpec(memory_space=pltpu.VMEM)] * (many + 2),
        out_specs=[pl.BlockSpec(memory_space=pltpu.VMEM)] * many,
        out_shape=[jax.ShapeDtypeStruct((tall, seg), BF)] * many,
        compiler_params=pltpu.CompilerParams(vmem_limit_bytes=24 * MIB),
        cost_estimate=pl.CostEstimate(
            flops=2 * height * seg * SEGS * units * 3,
            bytes_accessed=3 * 2 * units * seg * SEGS,
            transcendentals=0,
        ),
        name="experts",
    )(*blocks, both_weight, down_weight)


def combine(own_terms, twin, slot, scale):
    seg = twin.shape[1]
    count = slot.shape[2]
    terms = len(own_terms)

    def kernel(*refs):
        term_refs = refs[:terms]
        twin_ref, slot_ref, scale_ref, out_ref, stage, sems = refs[terms:]
        own = term_refs[0][0:ROWS].astype(F32)
        for ref in term_refs[1:]:
            own = own + ref[0:ROWS].astype(F32)
        own = own * scale_ref[0][:, 0:1]
        other = twin_ref[...].astype(F32) * scale_ref[1][:, 0:1]
        both = jnp.concatenate([own, other], axis=0)
        high = both.astype(BF)
        low = (both - high.astype(F32)).astype(BF)
        rows = jnp.concatenate([high, low], axis=0)
        table = jnp.concatenate([slot_ref[0], slot_ref[1]], axis=0)
        table = jnp.concatenate([table, table], axis=0).T
        line = lax.broadcasted_iota(jnp.int32, (count, 4 * ROWS), 1) % ROWS // MOST
        copies = []
        for s in range(SEGS):
            chosen = jnp.where(line == s, table, 0.0).astype(BF)
            stage[s] = jnp.dot(chosen, rows, preferred_element_type=F32).astype(BF)
            copy = pltpu.make_async_copy(
                stage.at[s], out_ref.at[:, pl.ds(s * seg, seg)], sems.at[s]
            )
            copy.start()
            copies.append(copy)
        for copy in copies:
            copy.wait()

    return pl.pallas_call(
        kernel,
        in_specs=[pl.BlockSpec(memory_space=pltpu.VMEM)] * (terms + 3),
        out_specs=pl.BlockSpec(memory_space=pltpu.HBM),
        out_shape=jax.ShapeDtypeStruct((count, seg * SEGS), BF),
        scratch_shapes=[
            pltpu.VMEM((SEGS, count, seg), BF),
            pltpu.SemaphoreType.DMA((SEGS,)),
        ],
        compiler_params=pltpu.CompilerParams(vmem_limit_bytes=16 * MIB),
        name="combine",
    )(*own_terms, twin, slot, scale)


def swap(x, mask):
    return lax.ppermute(x, "local", [(i, i ^ mask) for i in range(SPLIT)])


def swap_cores(x):
    return lax.ppermute(x, "hst", [(0, 1), (1, 0)])


def add(*terms):
    return sum(x.astype(F32) for x in terms).astype(BF)


def single(tokens, expert_ids, route_weights, gate_weight, up_weight, down_weight):
    core = lax.axis_index("hst").astype(jnp.int32).reshape(1)
    own, other, slot, scale = select_rows(core, tokens, expert_ids.T, route_weights.T)
    block = jnp.concatenate([own, swap_cores(other)], axis=0)
    loaded = load_weights(gate_weight, up_weight, down_weight)
    six, two, one, *loaded = join(swap(block, 6), swap(block, 2), swap(block, 1), *loaded)
    four, seven = join(swap(six, 2), swap(six, 1))
    five, three = swap(four, 1), swap(one, 2)
    part7, part6 = experts([seven, six], *loaded)
    part0, part1, part2 = experts([block, one, two], *loaded)
    part5, part4, part3 = experts([five, four, three], *loaded)
    half = add(part5, swap(part7, 2))
    far = swap(add(part4, swap(part6, 2), swap(half, 1)), 4)
    near = swap(add(part2, swap(part3, 1)), 2)
    terms = (part0, swap(part1, 1), near, far)
    back = sum(x[ROWS:].astype(F32) for x in terms)
    back = swap_cores(back.astype(BF))
    return combine(terms, back, slot, scale)


def solution(mesh):
    in_specs = (
        P(("groups", "hst", "local"), None),
        P(("groups", "hst", "local"), None),
        P(("groups", "hst", "local"), None),
        P(None, ("hst", "local")),
        P(None, ("hst", "local")),
        P(("hst", "local"), None),
    )
    out_specs = P(("groups", "hst", "local"), None)
    body = single if mesh.shape["local"] == SPLIT and mesh.shape["hst"] == 2 else general
    return jax.shard_map(
        body, mesh=mesh, in_specs=in_specs, out_specs=out_specs, check_vma=False
    )
```

```python
import jax
import jax.numpy as jnp
from jax import lax
from jax.experimental import pallas as pl
from jax.experimental.pallas import tpu as pltpu
from jax.sharding import PartitionSpec as P

SPLIT = 8
MOST = 6
SEGS = 4
ROWS = SEGS * MOST
BF = jnp.bfloat16
F32 = jnp.float32
MIB = 1024 * 1024
LATE = 8 * MIB


def route_table(expert_ids, route_weights, experts_win):
    window = jnp.arange(experts_win, dtype=jnp.int32)
    matched = expert_ids[:, :, None] == window[None, None, :]
    is_hit = jnp.any(matched, axis=1).astype(jnp.int32)
    weight = jnp.sum(jnp.where(matched, route_weights[:, :, None], F32(0.0)), axis=1)
    position = jnp.cumsum(is_hit, axis=0) - 1
    slot_index = jnp.arange(MOST, dtype=jnp.int32)
    select = (is_hit.T[:, None, :] == 1) & (position.T[:, None, :] == slot_index[None, :, None])
    return (select, weight)


def general(tokens, expert_ids, route_weights, gate_weight, up_weight, down_weight):
    host_count = lax.axis_size("hst")
    local_count = lax.axis_size("local")
    per_host = local_count // SPLIT
    experts_win = host_count * per_host
    width = tokens.shape[1]
    select, weight = route_table(expert_ids, route_weights, experts_win)
    outgoing = jnp.einsum(
        "wmt,td->wmd", select.astype(BF), tokens, preferred_element_type=F32
    ).astype(BF)
    slot_weight = jnp.einsum(
        "wmt,tw->wm", select.astype(F32), weight, precision=lax.Precision.HIGHEST
    )
    host_rows = lax.all_to_all(
        outgoing.reshape(host_count, per_host, MOST, width), "hst", 0, 0, tiled=True
    )
    spread = jnp.repeat(jnp.transpose(host_rows, (1, 0, 2, 3)), SPLIT, axis=0)
    row_block = lax.all_to_all(spread, "local", 0, 0, tiled=True)
    in_shape = row_block.shape
    flattened = row_block.reshape(-1, width)
    gate_sum = jnp.dot(flattened, gate_weight, preferred_element_type=F32)
    up_sum = jnp.dot(flattened, up_weight, preferred_element_type=F32)
    hidden = (jax.nn.silu(gate_sum) * up_sum).astype(BF)
    partial_value = jnp.dot(hidden, down_weight, preferred_element_type=F32).astype(BF)
    partial_value = partial_value.reshape(in_shape)
    returned_rows = lax.all_to_all(partial_value, "local", 0, 0, tiled=True)
    summed = jnp.sum(
        returned_rows.reshape(per_host, SPLIT, host_count, MOST, width).astype(F32), axis=1
    )
    returned_sums = lax.all_to_all(
        jnp.transpose(summed, (1, 0, 2, 3)), "hst", 0, 0, tiled=True
    )
    combined = returned_sums.reshape(experts_win, MOST, width)
    weighted = combined * slot_weight[:, :, None]
    total = jnp.einsum(
        "wmt,wmd->td", select.astype(F32), weighted, precision=lax.Precision.HIGHEST
    )
    return total.astype(BF)


def in_hbm(x):
    return pltpu.with_memory_space_constraint(x, pltpu.HBM)


def join(*arrays, cost=0):
    many = len(arrays)

    def kernel(*refs):
        pass

    return pl.pallas_call(
        kernel,
        in_specs=[pl.BlockSpec(memory_space=pltpu.VMEM)] * many,
        out_specs=[pl.BlockSpec(memory_space=pltpu.VMEM)] * many,
        out_shape=[jax.ShapeDtypeStruct(x.shape, x.dtype) for x in arrays],
        input_output_aliases={i: i for i in range(many)},
        compiler_params=pltpu.CompilerParams(vmem_limit_bytes=8 * MIB),
        cost_estimate=pl.CostEstimate(flops=0, bytes_accessed=cost, transcendentals=0),
        name="join",
    )(*arrays)


def load_weights(gate_weight, up_weight, down_weight):
    width, units = gate_weight.shape
    seg = width // SEGS

    def kernel(gate_hbm, up_hbm, down_hbm, both_ref, down_ref, sems):
        copies = [
            pltpu.make_async_copy(gate_hbm, both_ref.at[:, pl.ds(0, units)], sems.at[0]),
            pltpu.make_async_copy(up_hbm, both_ref.at[:, pl.ds(units, units)], sems.at[1]),
        ]
        for s in range(SEGS):
            copies.append(
                pltpu.make_async_copy(
                    down_hbm.at[:, pl.ds(s * seg, seg)],
                    down_ref.at[pl.ds(s * units, units), :],
                    sems.at[2 + s],
                )
            )
        for copy in copies:
            copy.start()
        for copy in copies:
            copy.wait()

    return pl.pallas_call(
        kernel,
        in_specs=[pl.BlockSpec(memory_space=pltpu.HBM)] * 3,
        out_specs=[pl.BlockSpec(memory_space=pltpu.VMEM)] * 2,
        out_shape=[
            jax.ShapeDtypeStruct((width, 2 * units), BF),
            jax.ShapeDtypeStruct((SEGS * units, seg), BF),
        ],
        scratch_shapes=[pltpu.SemaphoreType.DMA((2 + SEGS,))],
        compiler_params=pltpu.CompilerParams(vmem_limit_bytes=12 * MIB),
        name="load_weights",
    )(*[in_hbm(x) for x in (gate_weight, up_weight, down_weight)])


def select_rows(core, tokens, ids_t, weights_t):
    count, width = tokens.shape
    seg = width // SEGS
    topk = ids_t.shape[0]

    def kernel(
        core_ref, ids_hbm, weights_hbm, tokens_hbm,
        own_ref, twin_ref, slot_ref, scale_ref,
        ids_ref, weights_ref, tokens_ref, small_sem, sems,
    ):
        first = pltpu.make_async_copy(ids_hbm, ids_ref, small_sem.at[0])
        second = pltpu.make_async_copy(weights_hbm, weights_ref, small_sem.at[1])
        first.start()
        second.start()
        copies = [
            pltpu.make_async_copy(
                tokens_hbm.at[:, pl.ds(s * seg, seg)], tokens_ref.at[s], sems.at[s]
            )
            for s in range(SEGS)
        ]
        for copy in copies:
            copy.start()
        core = core_ref[0]
        row = lax.broadcasted_iota(jnp.int32, (count, count), 0)
        col = lax.broadcasted_iota(jnp.int32, (count, count), 1)
        before = (row < col).astype(BF)
        slot = lax.broadcasted_iota(jnp.int32, (ROWS, count), 0) % MOST
        line = lax.broadcasted_iota(jnp.int32, (2 * ROWS, count), 0) % ROWS // MOST
        first.wait()
        second.wait()
        ids = ids_ref[...]
        tables = []
        for part in range(2):
            expert = core if part == 0 else 1 - core
            named = ids == expert
            hit = jnp.max(named.astype(F32), axis=0, keepdims=True)
            weight = jnp.sum(jnp.where(named, weights_ref[...], 0.0), axis=0, keepdims=True)
            wide = jnp.broadcast_to(hit, (16, count)).astype(BF)
            position = jnp.dot(wide, before, preferred_element_type=F32)[0:1]
            table = ((hit > 0.0) & (position.astype(jnp.int32) == slot)).astype(F32)
            slot_ref[part] = table
            scale = jnp.sum(table * weight, axis=1, keepdims=True)
            scale_ref[part] = jnp.broadcast_to(scale, (ROWS, 128))
            tables.append(table)
        table = jnp.concatenate(tables, axis=0)
        rows = jnp.zeros((2 * ROWS, seg), F32)
        for s in range(SEGS):
            copies[s].wait()
            chosen = jnp.where(line == s, table, 0.0).astype(BF)
            rows = rows + jnp.dot(chosen, tokens_ref[s], preferred_element_type=F32)
        own_ref[...] = rows[:ROWS].astype(BF)
        twin_ref[...] = rows[ROWS:].astype(BF)

    return pl.pallas_call(
        kernel,
        in_specs=[pl.BlockSpec(memory_space=pltpu.SMEM)] + [pl.BlockSpec(memory_space=pltpu.HBM)] * 3,
        out_specs=[pl.BlockSpec(memory_space=pltpu.VMEM)] * 4,
        out_shape=[
            jax.ShapeDtypeStruct((ROWS, seg), BF),
            jax.ShapeDtypeStruct((ROWS, seg), BF),
            jax.ShapeDtypeStruct((2, ROWS, count), F32),
            jax.ShapeDtypeStruct((2, ROWS, 128), F32),
        ],
        scratch_shapes=[
            pltpu.VMEM((topk, count), jnp.int32),
            pltpu.VMEM((topk, count), F32),
            pltpu.VMEM((SEGS, count, seg), BF),
            pltpu.SemaphoreType.DMA((2,)),
            pltpu.SemaphoreType.DMA((SEGS,)),
        ],
        compiler_params=pltpu.CompilerParams(vmem_limit_bytes=12 * MIB),
        name="select_rows",
    )(core, *[in_hbm(x) for x in (ids_t, weights_t, tokens)])


def experts(blocks, both_weight, down_weight):
    many = len(blocks)
    tall, seg = blocks[0].shape
    units = both_weight.shape[1] // 2
    height = many * tall
    tile = 256

    def kernel(*refs):
        block_refs = refs[:many]
        both_ref, down_ref = refs[many : many + 2]
        out_refs = refs[many + 2 :]
        rows = jnp.concatenate([ref[...] for ref in block_refs], axis=0)
        line = lax.broadcasted_iota(jnp.int32, (height, 2 * units), 0) % ROWS // MOST
        total = jnp.zeros((height, 2 * units), F32)
        for s in range(SEGS):
            cut = slice(s * seg, (s + 1) * seg)
            part = jnp.dot(rows, both_ref[cut, :], preferred_element_type=F32)
            total = total + jnp.where(line == s, part, 0.0)
        one = lax.broadcasted_iota(jnp.int32, (tall, tall), 0)
        two = lax.broadcasted_iota(jnp.int32, (tall, tall), 1)
        same = ((one // ROWS == two // ROWS) & (one % MOST == two % MOST)).astype(F32)
        spread = jnp.concatenate(
            [
                jnp.dot(
                    same,
                    total[b * tall : (b + 1) * tall],
                    precision=lax.Precision.HIGHEST,
                    preferred_element_type=F32,
                )
                for b in range(many)
            ],
            axis=0,
        )
        gate = spread[:, :units]
        up = spread[:, units:]
        hidden = gate / (1.0 + jnp.exp(-gate)) * up
        wide = jnp.concatenate(
            [jnp.where(line[:, :units] == s, hidden, 0.0) for s in range(SEGS)], axis=1
        ).astype(BF)
        for j in range(seg // tile):
            cut = slice(j * tile, (j + 1) * tile)
            out = jnp.dot(wide, down_ref[:, cut], preferred_element_type=F32).astype(BF)
            for b in range(many):
                out_refs[b][:, cut] = out[b * tall : (b + 1) * tall]

    return pl.pallas_call(
        kernel,
        in_specs=[pl.BlockSpec(memory_space=pltpu.VMEM)] * (many + 2),
        out_specs=[pl.BlockSpec(memory_space=pltpu.VMEM)] * many,
        out_shape=[jax.ShapeDtypeStruct((tall, seg), BF)] * many,
        compiler_params=pltpu.CompilerParams(vmem_limit_bytes=24 * MIB),
        cost_estimate=pl.CostEstimate(
            flops=2 * height * seg * SEGS * units * 3,
            bytes_accessed=3 * 2 * units * seg * SEGS,
            transcendentals=0,
        ),
        name="experts",
    )(*blocks, both_weight, down_weight)


def combine(own_terms, twin, slot, scale):
    seg = twin.shape[1]
    count = slot.shape[2]
    terms = len(own_terms)

    def kernel(*refs):
        term_refs = refs[:terms]
        twin_ref, slot_ref, scale_ref, out_ref, stage, sems = refs[terms:]
        own = term_refs[0][0:ROWS].astype(F32)
        for ref in term_refs[1:]:
            own = own + ref[0:ROWS].astype(F32)
        own = own * scale_ref[0][:, 0:1]
        other = twin_ref[...].astype(F32) * scale_ref[1][:, 0:1]
        both = jnp.concatenate([own, other], axis=0)
        high = both.astype(BF)
        low = (both - high.astype(F32)).astype(BF)
        rows = jnp.concatenate([high, low], axis=0)
        table = jnp.concatenate([slot_ref[0], slot_ref[1]], axis=0)
        table = jnp.concatenate([table, table], axis=0).T
        line = lax.broadcasted_iota(jnp.int32, (count, 4 * ROWS), 1) % ROWS // MOST
        copies = []
        for s in range(SEGS):
            chosen = jnp.where(line == s, table, 0.0).astype(BF)
            stage[s] = jnp.dot(chosen, rows, preferred_element_type=F32).astype(BF)
            copy = pltpu.make_async_copy(
                stage.at[s], out_ref.at[:, pl.ds(s * seg, seg)], sems.at[s]
            )
            copy.start()
            copies.append(copy)
        for copy in copies:
            copy.wait()

    return pl.pallas_call(
        kernel,
        in_specs=[pl.BlockSpec(memory_space=pltpu.VMEM)] * (terms + 3),
        out_specs=pl.BlockSpec(memory_space=pltpu.HBM),
        out_shape=jax.ShapeDtypeStruct((count, seg * SEGS), BF),
        scratch_shapes=[
            pltpu.VMEM((SEGS, count, seg), BF),
            pltpu.SemaphoreType.DMA((SEGS,)),
        ],
        compiler_params=pltpu.CompilerParams(vmem_limit_bytes=16 * MIB),
        name="combine",
    )(*own_terms, twin, slot, scale)


def swap(x, mask):
    return lax.ppermute(x, "local", [(i, i ^ mask) for i in range(SPLIT)])


def swap_cores(x):
    return lax.ppermute(x, "hst", [(0, 1), (1, 0)])


def add(*terms):
    return sum(x.astype(F32) for x in terms).astype(BF)


def single(tokens, expert_ids, route_weights, gate_weight, up_weight, down_weight):
    core = lax.axis_index("hst").astype(jnp.int32).reshape(1)
    own, other, slot, scale = select_rows(core, tokens, expert_ids.T, route_weights.T)
    block = jnp.concatenate([own, swap_cores(other)], axis=0)
    loaded = load_weights(gate_weight, up_weight, down_weight)
    (six,) = join(swap(block, 6), cost=LATE)
    six, one, two, *loaded = join(six, swap(block, 1), swap(block, 2), *loaded)
    four, seven = join(swap(six, 2), swap(six, 1))
    five = swap(four, 1)
    (three,) = join(swap(one, 2), cost=3 * LATE)
    part7, part6 = experts([seven, six], *loaded)
    part0, part1, part2, part3 = experts([block, one, two, three], *loaded)
    part5, part4 = experts([five, four], *loaded)
    half = swap(add(part5, swap(part7, 2)), 1)
    half, part1 = join(half, part1)
    (other6,) = join(swap(part6, 2), cost=3 * LATE)
    (far,) = join(swap(add(part4, other6, half), 4), cost=2 * LATE)
    near = swap(add(part2, swap(part3, 1)), 2)
    terms = (part0, swap(part1, 1), near, far)
    back = sum(x[ROWS:].astype(F32) for x in terms)
    back = swap_cores(back.astype(BF))
    return combine(terms, back, slot, scale)


def solution(mesh):
    in_specs = (
        P(("groups", "hst", "local"), None),
        P(("groups", "hst", "local"), None),
        P(("groups", "hst", "local"), None),
        P(None, ("hst", "local")),
        P(None, ("hst", "local")),
        P(("hst", "local"), None),
    )
    out_specs = P(("groups", "hst", "local"), None)
    body = single if mesh.shape["local"] == SPLIT and mesh.shape["hst"] == 2 else general
    return jax.shard_map(
        body, mesh=mesh, in_specs=in_specs, out_specs=out_specs, check_vma=False
    )
```

```python
import jax
import jax.numpy as jnp
from jax import lax
from jax.experimental import pallas as pl
from jax.experimental.pallas import tpu as pltpu
from jax.sharding import PartitionSpec as P

SPLIT = 8
MOST = 6
SEGS = 4
ROWS = SEGS * MOST
BF = jnp.bfloat16
F32 = jnp.float32
MIB = 1024 * 1024
LATE = 8 * MIB


def route_table(expert_ids, route_weights, experts_win):
    window = jnp.arange(experts_win, dtype=jnp.int32)
    matched = expert_ids[:, :, None] == window[None, None, :]
    is_hit = jnp.any(matched, axis=1).astype(jnp.int32)
    weight = jnp.sum(jnp.where(matched, route_weights[:, :, None], F32(0.0)), axis=1)
    position = jnp.cumsum(is_hit, axis=0) - 1
    slot_index = jnp.arange(MOST, dtype=jnp.int32)
    select = (is_hit.T[:, None, :] == 1) & (position.T[:, None, :] == slot_index[None, :, None])
    return (select, weight)


def general(tokens, expert_ids, route_weights, gate_weight, up_weight, down_weight):
    host_count = lax.axis_size("hst")
    local_count = lax.axis_size("local")
    per_host = local_count // SPLIT
    experts_win = host_count * per_host
    width = tokens.shape[1]
    select, weight = route_table(expert_ids, route_weights, experts_win)
    outgoing = jnp.einsum(
        "wmt,td->wmd", select.astype(BF), tokens, preferred_element_type=F32
    ).astype(BF)
    slot_weight = jnp.einsum(
        "wmt,tw->wm", select.astype(F32), weight, precision=lax.Precision.HIGHEST
    )
    host_rows = lax.all_to_all(
        outgoing.reshape(host_count, per_host, MOST, width), "hst", 0, 0, tiled=True
    )
    spread = jnp.repeat(jnp.transpose(host_rows, (1, 0, 2, 3)), SPLIT, axis=0)
    row_block = lax.all_to_all(spread, "local", 0, 0, tiled=True)
    in_shape = row_block.shape
    flattened = row_block.reshape(-1, width)
    gate_sum = jnp.dot(flattened, gate_weight, preferred_element_type=F32)
    up_sum = jnp.dot(flattened, up_weight, preferred_element_type=F32)
    hidden = (jax.nn.silu(gate_sum) * up_sum).astype(BF)
    partial_value = jnp.dot(hidden, down_weight, preferred_element_type=F32).astype(BF)
    partial_value = partial_value.reshape(in_shape)
    returned_rows = lax.all_to_all(partial_value, "local", 0, 0, tiled=True)
    summed = jnp.sum(
        returned_rows.reshape(per_host, SPLIT, host_count, MOST, width).astype(F32), axis=1
    )
    returned_sums = lax.all_to_all(
        jnp.transpose(summed, (1, 0, 2, 3)), "hst", 0, 0, tiled=True
    )
    combined = returned_sums.reshape(experts_win, MOST, width)
    weighted = combined * slot_weight[:, :, None]
    total = jnp.einsum(
        "wmt,wmd->td", select.astype(F32), weighted, precision=lax.Precision.HIGHEST
    )
    return total.astype(BF)


def in_hbm(x):
    return pltpu.with_memory_space_constraint(x, pltpu.HBM)


def join(*arrays, cost=0):
    many = len(arrays)

    def kernel(*refs):
        pass

    return pl.pallas_call(
        kernel,
        in_specs=[pl.BlockSpec(memory_space=pltpu.VMEM)] * many,
        out_specs=[pl.BlockSpec(memory_space=pltpu.VMEM)] * many,
        out_shape=[jax.ShapeDtypeStruct(x.shape, x.dtype) for x in arrays],
        input_output_aliases={i: i for i in range(many)},
        compiler_params=pltpu.CompilerParams(vmem_limit_bytes=8 * MIB),
        cost_estimate=pl.CostEstimate(flops=0, bytes_accessed=cost, transcendentals=0),
        name="join",
    )(*arrays)


def load_weights(gate_weight, up_weight, down_weight):
    width, units = gate_weight.shape
    seg = width // SEGS

    def kernel(gate_hbm, up_hbm, down_hbm, both_ref, down_ref, sems):
        copies = [
            pltpu.make_async_copy(gate_hbm, both_ref.at[:, pl.ds(0, units)], sems.at[0]),
            pltpu.make_async_copy(up_hbm, both_ref.at[:, pl.ds(units, units)], sems.at[1]),
        ]
        for s in range(SEGS):
            copies.append(
                pltpu.make_async_copy(
                    down_hbm.at[:, pl.ds(s * seg, seg)],
                    down_ref.at[pl.ds(s * units, units), :],
                    sems.at[2 + s],
                )
            )
        for copy in copies:
            copy.start()
        for copy in copies:
            copy.wait()

    return pl.pallas_call(
        kernel,
        in_specs=[pl.BlockSpec(memory_space=pltpu.HBM)] * 3,
        out_specs=[pl.BlockSpec(memory_space=pltpu.VMEM)] * 2,
        out_shape=[
            jax.ShapeDtypeStruct((width, 2 * units), BF),
            jax.ShapeDtypeStruct((SEGS * units, seg), BF),
        ],
        scratch_shapes=[pltpu.SemaphoreType.DMA((2 + SEGS,))],
        compiler_params=pltpu.CompilerParams(vmem_limit_bytes=12 * MIB),
        name="load_weights",
    )(*[in_hbm(x) for x in (gate_weight, up_weight, down_weight)])


def select_rows(core, tokens, ids_t, weights_t):
    count, width = tokens.shape
    seg = width // SEGS
    topk = ids_t.shape[0]

    def kernel(
        core_ref, ids_hbm, weights_hbm, tokens_hbm,
        own_ref, twin_ref, slot_ref, scale_ref,
        ids_ref, weights_ref, tokens_ref, small_sem, sems,
    ):
        first = pltpu.make_async_copy(ids_hbm, ids_ref, small_sem.at[0])
        second = pltpu.make_async_copy(weights_hbm, weights_ref, small_sem.at[1])
        first.start()
        second.start()
        copies = [
            pltpu.make_async_copy(
                tokens_hbm.at[:, pl.ds(s * seg, seg)], tokens_ref.at[s], sems.at[s]
            )
            for s in range(SEGS)
        ]
        for copy in copies:
            copy.start()
        core = core_ref[0]
        row = lax.broadcasted_iota(jnp.int32, (count, count), 0)
        col = lax.broadcasted_iota(jnp.int32, (count, count), 1)
        before = (row < col).astype(BF)
        slot = lax.broadcasted_iota(jnp.int32, (ROWS, count), 0) % MOST
        line = lax.broadcasted_iota(jnp.int32, (2 * ROWS, count), 0) % ROWS // MOST
        first.wait()
        second.wait()
        ids = ids_ref[...]
        tables = []
        for part in range(2):
            expert = core if part == 0 else 1 - core
            named = ids == expert
            hit = jnp.max(named.astype(F32), axis=0, keepdims=True)
            weight = jnp.sum(jnp.where(named, weights_ref[...], 0.0), axis=0, keepdims=True)
            wide = jnp.broadcast_to(hit, (16, count)).astype(BF)
            position = jnp.dot(wide, before, preferred_element_type=F32)[0:1]
            table = ((hit > 0.0) & (position.astype(jnp.int32) == slot)).astype(F32)
            slot_ref[part] = table
            scale = jnp.sum(table * weight, axis=1, keepdims=True)
            scale_ref[part] = jnp.broadcast_to(scale, (ROWS, 128))
            tables.append(table)
        table = jnp.concatenate(tables, axis=0)
        rows = jnp.zeros((2 * ROWS, seg), F32)
        for s in range(SEGS):
            copies[s].wait()
            chosen = jnp.where(line == s, table, 0.0).astype(BF)
            rows = rows + jnp.dot(chosen, tokens_ref[s], preferred_element_type=F32)
        own_ref[...] = rows[:ROWS].astype(BF)
        twin_ref[...] = rows[ROWS:].astype(BF)

    return pl.pallas_call(
        kernel,
        in_specs=[pl.BlockSpec(memory_space=pltpu.SMEM)] + [pl.BlockSpec(memory_space=pltpu.HBM)] * 3,
        out_specs=[pl.BlockSpec(memory_space=pltpu.VMEM)] * 4,
        out_shape=[
            jax.ShapeDtypeStruct((ROWS, seg), BF),
            jax.ShapeDtypeStruct((ROWS, seg), BF),
            jax.ShapeDtypeStruct((2, ROWS, count), F32),
            jax.ShapeDtypeStruct((2, ROWS, 128), F32),
        ],
        scratch_shapes=[
            pltpu.VMEM((topk, count), jnp.int32),
            pltpu.VMEM((topk, count), F32),
            pltpu.VMEM((SEGS, count, seg), BF),
            pltpu.SemaphoreType.DMA((2,)),
            pltpu.SemaphoreType.DMA((SEGS,)),
        ],
        compiler_params=pltpu.CompilerParams(vmem_limit_bytes=12 * MIB),
        name="select_rows",
    )(core, *[in_hbm(x) for x in (ids_t, weights_t, tokens)])


def experts(blocks, both_weight, down_weight):
    many = len(blocks)
    tall, seg = blocks[0].shape
    units = both_weight.shape[1] // 2
    height = many * tall
    tile = 256

    def kernel(*refs):
        block_refs = refs[:many]
        both_ref, down_ref = refs[many : many + 2]
        out_refs = refs[many + 2 :]
        rows = jnp.concatenate([ref[...] for ref in block_refs], axis=0)
        line = lax.broadcasted_iota(jnp.int32, (height, 2 * units), 0) % ROWS // MOST
        total = jnp.zeros((height, 2 * units), F32)
        for s in range(SEGS):
            cut = slice(s * seg, (s + 1) * seg)
            part = jnp.dot(rows, both_ref[cut, :], preferred_element_type=F32)
            total = total + jnp.where(line == s, part, 0.0)
        high = total.astype(BF)
        low = (total - high.astype(F32)).astype(BF)
        one = lax.broadcasted_iota(jnp.int32, (height, 2 * height), 0)
        two = lax.broadcasted_iota(jnp.int32, (height, 2 * height), 1) % height
        same = ((one // ROWS == two // ROWS) & (one % MOST == two % MOST)).astype(BF)
        spread = jnp.dot(
            same, jnp.concatenate([high, low], axis=0), preferred_element_type=F32
        )
        gate = spread[:, :units]
        up = spread[:, units:]
        hidden = gate / (1.0 + jnp.exp(-gate)) * up
        wide = jnp.concatenate(
            [jnp.where(line[:, :units] == s, hidden, 0.0) for s in range(SEGS)], axis=1
        ).astype(BF)
        for j in range(seg // tile):
            cut = slice(j * tile, (j + 1) * tile)
            out = jnp.dot(wide, down_ref[:, cut], preferred_element_type=F32).astype(BF)
            for b in range(many):
                out_refs[b][:, cut] = out[b * tall : (b + 1) * tall]

    return pl.pallas_call(
        kernel,
        in_specs=[pl.BlockSpec(memory_space=pltpu.VMEM)] * (many + 2),
        out_specs=[pl.BlockSpec(memory_space=pltpu.VMEM)] * many,
        out_shape=[jax.ShapeDtypeStruct((tall, seg), BF)] * many,
        compiler_params=pltpu.CompilerParams(vmem_limit_bytes=24 * MIB),
        cost_estimate=pl.CostEstimate(
            flops=2 * height * seg * SEGS * units * 3,
            bytes_accessed=3 * 2 * units * seg * SEGS,
            transcendentals=0,
        ),
        name="experts",
    )(*blocks, both_weight, down_weight)


def combine(own_terms, twin, slot, scale):
    seg = twin.shape[1]
    count = slot.shape[2]
    terms = len(own_terms)

    def kernel(*refs):
        term_refs = refs[:terms]
        twin_ref, slot_ref, scale_ref, out_ref, stage, sems = refs[terms:]
        own = term_refs[0][0:ROWS].astype(F32)
        for ref in term_refs[1:]:
            own = own + ref[0:ROWS].astype(F32)
        own = own * scale_ref[0][:, 0:1]
        other = twin_ref[...].astype(F32) * scale_ref[1][:, 0:1]
        both = jnp.concatenate([own, other], axis=0)
        high = both.astype(BF)
        low = (both - high.astype(F32)).astype(BF)
        rows = jnp.concatenate([high, low], axis=0)
        table = jnp.concatenate([slot_ref[0], slot_ref[1]], axis=0)
        table = jnp.concatenate([table, table], axis=0).T
        line = lax.broadcasted_iota(jnp.int32, (count, 4 * ROWS), 1) % ROWS // MOST
        copies = []
        for s in range(SEGS):
            chosen = jnp.where(line == s, table, 0.0).astype(BF)
            stage[s] = jnp.dot(chosen, rows, preferred_element_type=F32).astype(BF)
            copy = pltpu.make_async_copy(
                stage.at[s], out_ref.at[:, pl.ds(s * seg, seg)], sems.at[s]
            )
            copy.start()
            copies.append(copy)
        for copy in copies:
            copy.wait()

    return pl.pallas_call(
        kernel,
        in_specs=[pl.BlockSpec(memory_space=pltpu.VMEM)] * (terms + 3),
        out_specs=pl.BlockSpec(memory_space=pltpu.HBM),
        out_shape=jax.ShapeDtypeStruct((count, seg * SEGS), BF),
        scratch_shapes=[
            pltpu.VMEM((SEGS, count, seg), BF),
            pltpu.SemaphoreType.DMA((SEGS,)),
        ],
        compiler_params=pltpu.CompilerParams(vmem_limit_bytes=16 * MIB),
        name="combine",
    )(*own_terms, twin, slot, scale)


def swap(x, mask):
    return lax.ppermute(x, "local", [(i, i ^ mask) for i in range(SPLIT)])


def swap_cores(x):
    return lax.ppermute(x, "hst", [(0, 1), (1, 0)])


def add(*terms):
    return sum(x.astype(F32) for x in terms).astype(BF)


def single(tokens, expert_ids, route_weights, gate_weight, up_weight, down_weight):
    core = lax.axis_index("hst").astype(jnp.int32).reshape(1)
    own, other, slot, scale = select_rows(core, tokens, expert_ids.T, route_weights.T)
    block = jnp.concatenate([own, swap_cores(other)], axis=0)
    loaded = load_weights(gate_weight, up_weight, down_weight)
    (six,) = join(swap(block, 6), cost=1 * LATE)
    six, one, two, *loaded = join(six, swap(block, 1), swap(block, 2), *loaded)
    (four,) = join(swap(six, 2), cost=1 * LATE)
    four, seven = join(four, swap(six, 1))
    five = swap(four, 1)
    (three,) = join(swap(one, 2), cost=3 * LATE)
    part7, part6, part4 = experts([seven, six, four], *loaded)
    part0, part1, part2, part3 = experts([block, one, two, three], *loaded)
    (part5,) = experts([five], *loaded)
    half = swap(add(part5, swap(part7, 2)), 1)
    half, part1 = join(half, part1)
    (other6,) = join(swap(part6, 2), cost=3 * LATE)
    (far,) = join(swap(add(part4, other6, half), 4), cost=2 * LATE)
    near = swap(add(part2, swap(part3, 1)), 2)
    terms = (part0, swap(part1, 1), near, far)
    back = sum(x[ROWS:].astype(F32) for x in terms)
    back = swap_cores(back.astype(BF))
    return combine(terms, back, slot, scale)


def solution(mesh):
    in_specs = (
        P(("groups", "hst", "local"), None),
        P(("groups", "hst", "local"), None),
        P(("groups", "hst", "local"), None),
        P(None, ("hst", "local")),
        P(None, ("hst", "local")),
        P(("hst", "local"), None),
    )
    out_specs = P(("groups", "hst", "local"), None)
    body = single if mesh.shape["local"] == SPLIT and mesh.shape["hst"] == 2 else general
    return jax.shard_map(
        body, mesh=mesh, in_specs=in_specs, out_specs=out_specs, check_vma=False
    )
```

```python
import jax
import jax.numpy as jnp
from jax import lax
from jax.experimental import pallas as pl
from jax.experimental.pallas import tpu as pltpu
from jax.sharding import PartitionSpec as P

SPLIT = 8
MOST = 6
SEGS = 4
ROWS = SEGS * MOST
BF = jnp.bfloat16
F32 = jnp.float32
MIB = 1024 * 1024
LATE = 8 * MIB


def route_table(expert_ids, route_weights, experts_win):
    window = jnp.arange(experts_win, dtype=jnp.int32)
    matched = expert_ids[:, :, None] == window[None, None, :]
    is_hit = jnp.any(matched, axis=1).astype(jnp.int32)
    weight = jnp.sum(jnp.where(matched, route_weights[:, :, None], F32(0.0)), axis=1)
    position = jnp.cumsum(is_hit, axis=0) - 1
    slot_index = jnp.arange(MOST, dtype=jnp.int32)
    select = (is_hit.T[:, None, :] == 1) & (position.T[:, None, :] == slot_index[None, :, None])
    return (select, weight)


def general(tokens, expert_ids, route_weights, gate_weight, up_weight, down_weight):
    host_count = lax.axis_size("hst")
    local_count = lax.axis_size("local")
    per_host = local_count // SPLIT
    experts_win = host_count * per_host
    width = tokens.shape[1]
    select, weight = route_table(expert_ids, route_weights, experts_win)
    outgoing = jnp.einsum(
        "wmt,td->wmd", select.astype(BF), tokens, preferred_element_type=F32
    ).astype(BF)
    slot_weight = jnp.einsum(
        "wmt,tw->wm", select.astype(F32), weight, precision=lax.Precision.HIGHEST
    )
    host_rows = lax.all_to_all(
        outgoing.reshape(host_count, per_host, MOST, width), "hst", 0, 0, tiled=True
    )
    spread = jnp.repeat(jnp.transpose(host_rows, (1, 0, 2, 3)), SPLIT, axis=0)
    row_block = lax.all_to_all(spread, "local", 0, 0, tiled=True)
    in_shape = row_block.shape
    flattened = row_block.reshape(-1, width)
    gate_sum = jnp.dot(flattened, gate_weight, preferred_element_type=F32)
    up_sum = jnp.dot(flattened, up_weight, preferred_element_type=F32)
    hidden = (jax.nn.silu(gate_sum) * up_sum).astype(BF)
    partial_value = jnp.dot(hidden, down_weight, preferred_element_type=F32).astype(BF)
    partial_value = partial_value.reshape(in_shape)
    returned_rows = lax.all_to_all(partial_value, "local", 0, 0, tiled=True)
    summed = jnp.sum(
        returned_rows.reshape(per_host, SPLIT, host_count, MOST, width).astype(F32), axis=1
    )
    returned_sums = lax.all_to_all(
        jnp.transpose(summed, (1, 0, 2, 3)), "hst", 0, 0, tiled=True
    )
    combined = returned_sums.reshape(experts_win, MOST, width)
    weighted = combined * slot_weight[:, :, None]
    total = jnp.einsum(
        "wmt,wmd->td", select.astype(F32), weighted, precision=lax.Precision.HIGHEST
    )
    return total.astype(BF)


def in_hbm(x):
    return pltpu.with_memory_space_constraint(x, pltpu.HBM)


def join(*arrays, cost=0):
    many = len(arrays)

    def kernel(*refs):
        pass

    return pl.pallas_call(
        kernel,
        in_specs=[pl.BlockSpec(memory_space=pltpu.VMEM)] * many,
        out_specs=[pl.BlockSpec(memory_space=pltpu.VMEM)] * many,
        out_shape=[jax.ShapeDtypeStruct(x.shape, x.dtype) for x in arrays],
        input_output_aliases={i: i for i in range(many)},
        compiler_params=pltpu.CompilerParams(vmem_limit_bytes=8 * MIB),
        cost_estimate=pl.CostEstimate(flops=0, bytes_accessed=cost, transcendentals=0),
        name="join",
    )(*arrays)


def load_weights(gate_weight, up_weight, down_weight):
    width, units = gate_weight.shape
    seg = width // SEGS

    def kernel(gate_hbm, up_hbm, down_hbm, both_ref, down_ref, sems):
        copies = [
            pltpu.make_async_copy(gate_hbm, both_ref.at[:, pl.ds(0, units)], sems.at[0]),
            pltpu.make_async_copy(up_hbm, both_ref.at[:, pl.ds(units, units)], sems.at[1]),
        ]
        for s in range(SEGS):
            copies.append(
                pltpu.make_async_copy(
                    down_hbm.at[:, pl.ds(s * seg, seg)],
                    down_ref.at[pl.ds(s * units, units), :],
                    sems.at[2 + s],
                )
            )
        for copy in copies:
            copy.start()
        for copy in copies:
            copy.wait()

    return pl.pallas_call(
        kernel,
        in_specs=[pl.BlockSpec(memory_space=pltpu.HBM)] * 3,
        out_specs=[pl.BlockSpec(memory_space=pltpu.VMEM)] * 2,
        out_shape=[
            jax.ShapeDtypeStruct((width, 2 * units), BF),
            jax.ShapeDtypeStruct((SEGS * units, seg), BF),
        ],
        scratch_shapes=[pltpu.SemaphoreType.DMA((2 + SEGS,))],
        compiler_params=pltpu.CompilerParams(vmem_limit_bytes=12 * MIB),
        name="load_weights",
    )(*[in_hbm(x) for x in (gate_weight, up_weight, down_weight)])


def select_rows(core, tokens, ids_t, weights_t):
    count, width = tokens.shape
    seg = width // SEGS
    topk = ids_t.shape[0]

    def kernel(
        core_ref, ids_hbm, weights_hbm, tokens_hbm,
        own_ref, twin_ref, slot_ref, scale_ref,
        ids_ref, weights_ref, tokens_ref, small_sem, sems,
    ):
        first = pltpu.make_async_copy(ids_hbm, ids_ref, small_sem.at[0])
        second = pltpu.make_async_copy(weights_hbm, weights_ref, small_sem.at[1])
        first.start()
        second.start()
        copies = [
            pltpu.make_async_copy(
                tokens_hbm.at[:, pl.ds(s * seg, seg)], tokens_ref.at[s], sems.at[s]
            )
            for s in range(SEGS)
        ]
        for copy in copies:
            copy.start()
        core = core_ref[0]
        row = lax.broadcasted_iota(jnp.int32, (count, count), 0)
        col = lax.broadcasted_iota(jnp.int32, (count, count), 1)
        before = (row < col).astype(BF)
        slot = lax.broadcasted_iota(jnp.int32, (ROWS, count), 0) % MOST
        line = lax.broadcasted_iota(jnp.int32, (2 * ROWS, count), 0) % ROWS // MOST
        first.wait()
        second.wait()
        ids = ids_ref[...]
        tables = []
        for part in range(2):
            expert = core if part == 0 else 1 - core
            named = ids == expert
            hit = jnp.max(named.astype(F32), axis=0, keepdims=True)
            weight = jnp.sum(jnp.where(named, weights_ref[...], 0.0), axis=0, keepdims=True)
            wide = jnp.broadcast_to(hit, (16, count)).astype(BF)
            position = jnp.dot(wide, before, preferred_element_type=F32)[0:1]
            table = ((hit > 0.0) & (position.astype(jnp.int32) == slot)).astype(F32)
            slot_ref[part] = table
            scale = jnp.sum(table * weight, axis=1, keepdims=True)
            scale_ref[part] = jnp.broadcast_to(scale, (ROWS, 128))
            tables.append(table)
        table = jnp.concatenate(tables, axis=0)
        rows = jnp.zeros((2 * ROWS, seg), F32)
        for s in range(SEGS):
            copies[s].wait()
            chosen = jnp.where(line == s, table, 0.0).astype(BF)
            rows = rows + jnp.dot(chosen, tokens_ref[s], preferred_element_type=F32)
        own_ref[...] = rows[:ROWS].astype(BF)
        twin_ref[...] = rows[ROWS:].astype(BF)

    return pl.pallas_call(
        kernel,
        in_specs=[pl.BlockSpec(memory_space=pltpu.SMEM)] + [pl.BlockSpec(memory_space=pltpu.HBM)] * 3,
        out_specs=[pl.BlockSpec(memory_space=pltpu.VMEM)] * 4,
        out_shape=[
            jax.ShapeDtypeStruct((ROWS, seg), BF),
            jax.ShapeDtypeStruct((ROWS, seg), BF),
            jax.ShapeDtypeStruct((2, ROWS, count), F32),
            jax.ShapeDtypeStruct((2, ROWS, 128), F32),
        ],
        scratch_shapes=[
            pltpu.VMEM((topk, count), jnp.int32),
            pltpu.VMEM((topk, count), F32),
            pltpu.VMEM((SEGS, count, seg), BF),
            pltpu.SemaphoreType.DMA((2,)),
            pltpu.SemaphoreType.DMA((SEGS,)),
        ],
        compiler_params=pltpu.CompilerParams(vmem_limit_bytes=12 * MIB),
        name="select_rows",
    )(core, *[in_hbm(x) for x in (ids_t, weights_t, tokens)])


def experts(blocks, both_weight, down_weight):
    many = len(blocks)
    tall, seg = blocks[0].shape
    units = both_weight.shape[1] // 2
    height = many * tall
    tile = 256

    def kernel(*refs):
        block_refs = refs[:many]
        both_ref, down_ref = refs[many : many + 2]
        out_refs = refs[many + 2 :]
        rows = jnp.concatenate([ref[...] for ref in block_refs], axis=0)
        line = lax.broadcasted_iota(jnp.int32, (height, 2 * units), 0) % ROWS // MOST
        total = jnp.zeros((height, 2 * units), F32)
        for s in range(SEGS):
            cut = slice(s * seg, (s + 1) * seg)
            part = jnp.dot(rows, both_ref[cut, :], preferred_element_type=F32)
            total = total + jnp.where(line == s, part, 0.0)
        high = total.astype(BF)
        low = (total - high.astype(F32)).astype(BF)
        one = lax.broadcasted_iota(jnp.int32, (height, 2 * height), 0)
        two = lax.broadcasted_iota(jnp.int32, (height, 2 * height), 1) % height
        same = ((one // ROWS == two // ROWS) & (one % MOST == two % MOST)).astype(BF)
        spread = jnp.dot(
            same, jnp.concatenate([high, low], axis=0), preferred_element_type=F32
        )
        gate = spread[:, :units]
        up = spread[:, units:]
        hidden = gate / (1.0 + jnp.exp(-gate)) * up
        wide = jnp.concatenate(
            [jnp.where(line[:, :units] == s, hidden, 0.0) for s in range(SEGS)], axis=1
        ).astype(BF)
        for j in range(seg // tile):
            cut = slice(j * tile, (j + 1) * tile)
            out = jnp.dot(wide, down_ref[:, cut], preferred_element_type=F32).astype(BF)
            for b in range(many):
                out_refs[b][:, cut] = out[b * tall : (b + 1) * tall]

    return pl.pallas_call(
        kernel,
        in_specs=[pl.BlockSpec(memory_space=pltpu.VMEM)] * (many + 2),
        out_specs=[pl.BlockSpec(memory_space=pltpu.VMEM)] * many,
        out_shape=[jax.ShapeDtypeStruct((tall, seg), BF)] * many,
        compiler_params=pltpu.CompilerParams(vmem_limit_bytes=24 * MIB),
        cost_estimate=pl.CostEstimate(
            flops=2 * height * seg * SEGS * units * 3,
            bytes_accessed=3 * 2 * units * seg * SEGS,
            transcendentals=0,
        ),
        name="experts",
    )(*blocks, both_weight, down_weight)


def combine(own_terms, twin, slot, scale):
    seg = twin.shape[1]
    count = slot.shape[2]
    terms = len(own_terms)

    def kernel(*refs):
        term_refs = refs[:terms]
        twin_ref, slot_ref, scale_ref, out_ref, stage, sems = refs[terms:]
        own = term_refs[0][0:ROWS].astype(F32)
        for ref in term_refs[1:]:
            own = own + ref[0:ROWS].astype(F32)
        own = own * scale_ref[0][:, 0:1]
        other = twin_ref[...].astype(F32) * scale_ref[1][:, 0:1]
        both = jnp.concatenate([own, other], axis=0)
        high = both.astype(BF)
        low = (both - high.astype(F32)).astype(BF)
        rows = jnp.concatenate([high, low], axis=0)
        table = jnp.concatenate([slot_ref[0], slot_ref[1]], axis=0)
        table = jnp.concatenate([table, table], axis=0).T
        line = lax.broadcasted_iota(jnp.int32, (count, 4 * ROWS), 1) % ROWS // MOST
        copies = []
        for s in range(SEGS):
            chosen = jnp.where(line == s, table, 0.0).astype(BF)
            stage[s] = jnp.dot(chosen, rows, preferred_element_type=F32).astype(BF)
            copy = pltpu.make_async_copy(
                stage.at[s], out_ref.at[:, pl.ds(s * seg, seg)], sems.at[s]
            )
            copy.start()
            copies.append(copy)
        for copy in copies:
            copy.wait()

    return pl.pallas_call(
        kernel,
        in_specs=[pl.BlockSpec(memory_space=pltpu.VMEM)] * (terms + 3),
        out_specs=pl.BlockSpec(memory_space=pltpu.HBM),
        out_shape=jax.ShapeDtypeStruct((count, seg * SEGS), BF),
        scratch_shapes=[
            pltpu.VMEM((SEGS, count, seg), BF),
            pltpu.SemaphoreType.DMA((SEGS,)),
        ],
        compiler_params=pltpu.CompilerParams(vmem_limit_bytes=16 * MIB),
        name="combine",
    )(*own_terms, twin, slot, scale)


def swap(x, mask):
    return lax.ppermute(x, "local", [(i, i ^ mask) for i in range(SPLIT)])


def swap_cores(x):
    return lax.ppermute(x, "hst", [(0, 1), (1, 0)])


def add(*terms):
    return sum(x.astype(F32) for x in terms).astype(BF)


def single(tokens, expert_ids, route_weights, gate_weight, up_weight, down_weight):
    core = lax.axis_index("hst").astype(jnp.int32).reshape(1)
    own, other, slot, scale = select_rows(core, tokens, expert_ids.T, route_weights.T)
    block = jnp.concatenate([own, swap_cores(other)], axis=0)
    loaded = load_weights(gate_weight, up_weight, down_weight)
    (six,) = join(swap(block, 6), cost=1 * LATE)
    one = swap(block, 1)
    six, two, *loaded = join(six, swap(block, 2), *loaded)
    (four,) = join(swap(six, 2), cost=1 * LATE)
    four, seven = join(four, swap(six, 1))
    five = swap(four, 1)
    (three,) = join(swap(one, 2), cost=3 * LATE)
    part7, part6, part4 = experts([seven, six, four], *loaded)
    part0, part1, part2, part3 = experts([block, one, two, three], *loaded)
    (part5,) = experts([five], *loaded)
    half = swap(add(part5, swap(part7, 2)), 1)
    half, part1 = join(half, part1)
    (other6,) = join(swap(part6, 2), cost=3 * LATE)
    (far,) = join(swap(add(part4, other6, half), 4), cost=2 * LATE)
    near = swap(add(part2, swap(part3, 1)), 2)
    terms = (part0, swap(part1, 1), near, far)
    back = sum(x[ROWS:].astype(F32) for x in terms)
    back = swap_cores(back.astype(BF))
    return combine(terms, back, slot, scale)


def solution(mesh):
    in_specs = (
        P(("groups", "hst", "local"), None),
        P(("groups", "hst", "local"), None),
        P(("groups", "hst", "local"), None),
        P(None, ("hst", "local")),
        P(None, ("hst", "local")),
        P(("hst", "local"), None),
    )
    out_specs = P(("groups", "hst", "local"), None)
    body = single if mesh.shape["local"] == SPLIT and mesh.shape["hst"] == 2 else general
    return jax.shard_map(
        body, mesh=mesh, in_specs=in_specs, out_specs=out_specs, check_vma=False
    )
```

```python
import jax
import jax.numpy as jnp
from jax import lax
from jax.experimental import pallas as pl
from jax.experimental.pallas import tpu as pltpu
from jax.sharding import PartitionSpec as P

SPLIT = 8
MOST = 6
SEGS = 4
ROWS = SEGS * MOST
BF = jnp.bfloat16
F32 = jnp.float32
MIB = 1024 * 1024
LATE = 8 * MIB


def route_table(expert_ids, route_weights, experts_win):
    window = jnp.arange(experts_win, dtype=jnp.int32)
    matched = expert_ids[:, :, None] == window[None, None, :]
    is_hit = jnp.any(matched, axis=1).astype(jnp.int32)
    weight = jnp.sum(jnp.where(matched, route_weights[:, :, None], F32(0.0)), axis=1)
    position = jnp.cumsum(is_hit, axis=0) - 1
    slot_index = jnp.arange(MOST, dtype=jnp.int32)
    select = (is_hit.T[:, None, :] == 1) & (position.T[:, None, :] == slot_index[None, :, None])
    return (select, weight)


def general(tokens, expert_ids, route_weights, gate_weight, up_weight, down_weight):
    host_count = lax.axis_size("hst")
    local_count = lax.axis_size("local")
    per_host = local_count // SPLIT
    experts_win = host_count * per_host
    width = tokens.shape[1]
    select, weight = route_table(expert_ids, route_weights, experts_win)
    outgoing = jnp.einsum(
        "wmt,td->wmd", select.astype(BF), tokens, preferred_element_type=F32
    ).astype(BF)
    slot_weight = jnp.einsum(
        "wmt,tw->wm", select.astype(F32), weight, precision=lax.Precision.HIGHEST
    )
    host_rows = lax.all_to_all(
        outgoing.reshape(host_count, per_host, MOST, width), "hst", 0, 0, tiled=True
    )
    spread = jnp.repeat(jnp.transpose(host_rows, (1, 0, 2, 3)), SPLIT, axis=0)
    row_block = lax.all_to_all(spread, "local", 0, 0, tiled=True)
    in_shape = row_block.shape
    flattened = row_block.reshape(-1, width)
    gate_sum = jnp.dot(flattened, gate_weight, preferred_element_type=F32)
    up_sum = jnp.dot(flattened, up_weight, preferred_element_type=F32)
    hidden = (jax.nn.silu(gate_sum) * up_sum).astype(BF)
    partial_value = jnp.dot(hidden, down_weight, preferred_element_type=F32).astype(BF)
    partial_value = partial_value.reshape(in_shape)
    returned_rows = lax.all_to_all(partial_value, "local", 0, 0, tiled=True)
    summed = jnp.sum(
        returned_rows.reshape(per_host, SPLIT, host_count, MOST, width).astype(F32), axis=1
    )
    returned_sums = lax.all_to_all(
        jnp.transpose(summed, (1, 0, 2, 3)), "hst", 0, 0, tiled=True
    )
    combined = returned_sums.reshape(experts_win, MOST, width)
    weighted = combined * slot_weight[:, :, None]
    total = jnp.einsum(
        "wmt,wmd->td", select.astype(F32), weighted, precision=lax.Precision.HIGHEST
    )
    return total.astype(BF)


def in_hbm(x):
    return pltpu.with_memory_space_constraint(x, pltpu.HBM)


def join(*arrays, cost=0):
    many = len(arrays)

    def kernel(*refs):
        pass

    return pl.pallas_call(
        kernel,
        in_specs=[pl.BlockSpec(memory_space=pltpu.VMEM)] * many,
        out_specs=[pl.BlockSpec(memory_space=pltpu.VMEM)] * many,
        out_shape=[jax.ShapeDtypeStruct(x.shape, x.dtype) for x in arrays],
        input_output_aliases={i: i for i in range(many)},
        compiler_params=pltpu.CompilerParams(vmem_limit_bytes=8 * MIB),
        cost_estimate=pl.CostEstimate(flops=0, bytes_accessed=cost, transcendentals=0),
        name="join",
    )(*arrays)


def load_weights(gate_weight, up_weight, down_weight):
    width, units = gate_weight.shape
    seg = width // SEGS

    def kernel(gate_hbm, up_hbm, down_hbm, both_ref, down_ref, sems):
        copies = [
            pltpu.make_async_copy(gate_hbm, both_ref.at[:, pl.ds(0, units)], sems.at[0]),
            pltpu.make_async_copy(up_hbm, both_ref.at[:, pl.ds(units, units)], sems.at[1]),
        ]
        for s in range(SEGS):
            copies.append(
                pltpu.make_async_copy(
                    down_hbm.at[:, pl.ds(s * seg, seg)],
                    down_ref.at[pl.ds(s * units, units), :],
                    sems.at[2 + s],
                )
            )
        for copy in copies:
            copy.start()
        for copy in copies:
            copy.wait()

    return pl.pallas_call(
        kernel,
        in_specs=[pl.BlockSpec(memory_space=pltpu.HBM)] * 3,
        out_specs=[pl.BlockSpec(memory_space=pltpu.VMEM)] * 2,
        out_shape=[
            jax.ShapeDtypeStruct((width, 2 * units), BF),
            jax.ShapeDtypeStruct((SEGS * units, seg), BF),
        ],
        scratch_shapes=[pltpu.SemaphoreType.DMA((2 + SEGS,))],
        compiler_params=pltpu.CompilerParams(vmem_limit_bytes=12 * MIB),
        name="load_weights",
    )(*[in_hbm(x) for x in (gate_weight, up_weight, down_weight)])


def select_rows(core, tokens, ids_t, weights_t):
    count, width = tokens.shape
    seg = width // SEGS
    topk = ids_t.shape[0]

    def kernel(
        core_ref, ids_hbm, weights_hbm, tokens_hbm,
        own_ref, twin_ref, slot_ref, scale_ref,
        ids_ref, weights_ref, tokens_ref, small_sem, sems,
    ):
        first = pltpu.make_async_copy(ids_hbm, ids_ref, small_sem.at[0])
        second = pltpu.make_async_copy(weights_hbm, weights_ref, small_sem.at[1])
        first.start()
        second.start()
        copies = [
            pltpu.make_async_copy(
                tokens_hbm.at[:, pl.ds(s * seg, seg)], tokens_ref.at[s], sems.at[s]
            )
            for s in range(SEGS)
        ]
        for copy in copies:
            copy.start()
        core = core_ref[0]
        row = lax.broadcasted_iota(jnp.int32, (count, count), 0)
        col = lax.broadcasted_iota(jnp.int32, (count, count), 1)
        before = (row < col).astype(BF)
        slot = lax.broadcasted_iota(jnp.int32, (ROWS, count), 0) % MOST
        line = lax.broadcasted_iota(jnp.int32, (2 * ROWS, count), 0) % ROWS // MOST
        first.wait()
        second.wait()
        ids = ids_ref[...]
        tables = []
        for part in range(2):
            expert = core if part == 0 else 1 - core
            named = ids == expert
            hit = jnp.max(named.astype(F32), axis=0, keepdims=True)
            weight = jnp.sum(jnp.where(named, weights_ref[...], 0.0), axis=0, keepdims=True)
            wide = jnp.broadcast_to(hit, (16, count)).astype(BF)
            position = jnp.dot(wide, before, preferred_element_type=F32)[0:1]
            table = ((hit > 0.0) & (position.astype(jnp.int32) == slot)).astype(F32)
            slot_ref[part] = table
            scale = jnp.sum(table * weight, axis=1, keepdims=True)
            scale_ref[part] = jnp.broadcast_to(scale, (ROWS, 128))
            tables.append(table)
        table = jnp.concatenate(tables, axis=0)
        rows = jnp.zeros((2 * ROWS, seg), F32)
        for s in range(SEGS):
            copies[s].wait()
            chosen = jnp.where(line == s, table, 0.0).astype(BF)
            rows = rows + jnp.dot(chosen, tokens_ref[s], preferred_element_type=F32)
        own_ref[...] = rows[:ROWS].astype(BF)
        twin_ref[...] = rows[ROWS:].astype(BF)

    return pl.pallas_call(
        kernel,
        in_specs=[pl.BlockSpec(memory_space=pltpu.SMEM)] + [pl.BlockSpec(memory_space=pltpu.HBM)] * 3,
        out_specs=[pl.BlockSpec(memory_space=pltpu.VMEM)] * 4,
        out_shape=[
            jax.ShapeDtypeStruct((ROWS, seg), BF),
            jax.ShapeDtypeStruct((ROWS, seg), BF),
            jax.ShapeDtypeStruct((2, ROWS, count), F32),
            jax.ShapeDtypeStruct((2, ROWS, 128), F32),
        ],
        scratch_shapes=[
            pltpu.VMEM((topk, count), jnp.int32),
            pltpu.VMEM((topk, count), F32),
            pltpu.VMEM((SEGS, count, seg), BF),
            pltpu.SemaphoreType.DMA((2,)),
            pltpu.SemaphoreType.DMA((SEGS,)),
        ],
        compiler_params=pltpu.CompilerParams(vmem_limit_bytes=12 * MIB),
        name="select_rows",
    )(core, *[in_hbm(x) for x in (ids_t, weights_t, tokens)])


def experts(blocks, both_weight, down_weight):
    many = len(blocks)
    tall, seg = blocks[0].shape
    units = both_weight.shape[1] // 2
    height = many * tall
    tile = 256

    def kernel(*refs):
        block_refs = refs[:many]
        both_ref, down_ref = refs[many : many + 2]
        out_refs = refs[many + 2 :]
        rows = jnp.concatenate([ref[...] for ref in block_refs], axis=0)
        line = lax.broadcasted_iota(jnp.int32, (height, 2 * units), 0) % ROWS // MOST
        total = jnp.zeros((height, 2 * units), F32)
        for s in range(SEGS):
            cut = slice(s * seg, (s + 1) * seg)
            part = jnp.dot(rows, both_ref[cut, :], preferred_element_type=F32)
            total = total + jnp.where(line == s, part, 0.0)
        high = total.astype(BF)
        low = (total - high.astype(F32)).astype(BF)
        one = lax.broadcasted_iota(jnp.int32, (height, 2 * height), 0)
        two = lax.broadcasted_iota(jnp.int32, (height, 2 * height), 1) % height
        same = ((one // ROWS == two // ROWS) & (one % MOST == two % MOST)).astype(BF)
        spread = jnp.dot(
            same, jnp.concatenate([high, low], axis=0), preferred_element_type=F32
        )
        gate = spread[:, :units]
        up = spread[:, units:]
        hidden = gate / (1.0 + jnp.exp(-gate)) * up
        wide = jnp.concatenate(
            [jnp.where(line[:, :units] == s, hidden, 0.0) for s in range(SEGS)], axis=1
        ).astype(BF)
        for j in range(seg // tile):
            cut = slice(j * tile, (j + 1) * tile)
            out = jnp.dot(wide, down_ref[:, cut], preferred_element_type=F32).astype(BF)
            for b in range(many):
                out_refs[b][:, cut] = out[b * tall : (b + 1) * tall]

    return pl.pallas_call(
        kernel,
        in_specs=[pl.BlockSpec(memory_space=pltpu.VMEM)] * (many + 2),
        out_specs=[pl.BlockSpec(memory_space=pltpu.VMEM)] * many,
        out_shape=[jax.ShapeDtypeStruct((tall, seg), BF)] * many,
        compiler_params=pltpu.CompilerParams(vmem_limit_bytes=24 * MIB),
        cost_estimate=pl.CostEstimate(
            flops=2 * height * seg * SEGS * units * 3,
            bytes_accessed=3 * 2 * units * seg * SEGS,
            transcendentals=0,
        ),
        name="experts",
    )(*blocks, both_weight, down_weight)


def combine(own_terms, twin, slot, scale):
    seg = twin.shape[1]
    count = slot.shape[2]
    terms = len(own_terms)

    def kernel(*refs):
        term_refs = refs[:terms]
        twin_ref, slot_ref, scale_ref, out_ref, stage, sems = refs[terms:]
        own = term_refs[0][0:ROWS].astype(F32)
        for ref in term_refs[1:]:
            own = own + ref[0:ROWS].astype(F32)
        own = own * scale_ref[0][:, 0:1]
        other = twin_ref[...].astype(F32) * scale_ref[1][:, 0:1]
        both = jnp.concatenate([own, other], axis=0)
        high = both.astype(BF)
        low = (both - high.astype(F32)).astype(BF)
        rows = jnp.concatenate([high, low], axis=0)
        table = jnp.concatenate([slot_ref[0], slot_ref[1]], axis=0)
        table = jnp.concatenate([table, table], axis=0).T
        line = lax.broadcasted_iota(jnp.int32, (count, 4 * ROWS), 1) % ROWS // MOST
        copies = []
        for s in range(SEGS):
            chosen = jnp.where(line == s, table, 0.0).astype(BF)
            stage[s] = jnp.dot(chosen, rows, preferred_element_type=F32).astype(BF)
            copy = pltpu.make_async_copy(
                stage.at[s], out_ref.at[:, pl.ds(s * seg, seg)], sems.at[s]
            )
            copy.start()
            copies.append(copy)
        for copy in copies:
            copy.wait()

    return pl.pallas_call(
        kernel,
        in_specs=[pl.BlockSpec(memory_space=pltpu.VMEM)] * (terms + 3),
        out_specs=pl.BlockSpec(memory_space=pltpu.HBM),
        out_shape=jax.ShapeDtypeStruct((count, seg * SEGS), BF),
        scratch_shapes=[
            pltpu.VMEM((SEGS, count, seg), BF),
            pltpu.SemaphoreType.DMA((SEGS,)),
        ],
        compiler_params=pltpu.CompilerParams(vmem_limit_bytes=16 * MIB),
        name="combine",
    )(*own_terms, twin, slot, scale)


def swap(x, mask):
    return lax.ppermute(x, "local", [(i, i ^ mask) for i in range(SPLIT)])


def swap_cores(x):
    return lax.ppermute(x, "hst", [(0, 1), (1, 0)])


def add(*terms):
    return sum(x.astype(F32) for x in terms).astype(BF)


def single(tokens, expert_ids, route_weights, gate_weight, up_weight, down_weight):
    core = lax.axis_index("hst").astype(jnp.int32).reshape(1)
    own, other, slot, scale = select_rows(core, tokens, expert_ids.T, route_weights.T)
    block = jnp.concatenate([own, swap_cores(other)], axis=0)
    loaded = load_weights(gate_weight, up_weight, down_weight)
    (six,) = join(swap(block, 6), cost=1 * LATE)
    one = swap(block, 1)
    six, two, *loaded = join(six, swap(block, 2), *loaded)
    (four,) = join(swap(six, 2), cost=1 * LATE)
    part0, part1, part2 = experts([block, one, two], *loaded)
    four, seven, part0 = join(four, swap(six, 1), part0)
    five = swap(four, 1)
    (three,) = join(swap(one, 2), cost=3 * LATE)
    part7, part6, part4 = experts([seven, six, four], *loaded)
    (part3,) = experts([three], *loaded)
    (part5,) = experts([five], *loaded)
    half = swap(add(part5, swap(part7, 2)), 1)
    half, part1 = join(half, part1)
    (other6,) = join(swap(part6, 2), cost=3 * LATE)
    (far,) = join(swap(add(part4, other6, half), 4), cost=2 * LATE)
    near = swap(add(part2, swap(part3, 1)), 2)
    terms = (part0, swap(part1, 1), near, far)
    back = sum(x[ROWS:].astype(F32) for x in terms)
    back = swap_cores(back.astype(BF))
    return combine(terms, back, slot, scale)


def solution(mesh):
    in_specs = (
        P(("groups", "hst", "local"), None),
        P(("groups", "hst", "local"), None),
        P(("groups", "hst", "local"), None),
        P(None, ("hst", "local")),
        P(None, ("hst", "local")),
        P(("hst", "local"), None),
    )
    out_specs = P(("groups", "hst", "local"), None)
    body = single if mesh.shape["local"] == SPLIT and mesh.shape["hst"] == 2 else general
    return jax.shard_map(
        body, mesh=mesh, in_specs=in_specs, out_specs=out_specs, check_vma=False
    )
```
